256 devices in a mesh: users: 16 (over x, y), items: 16 (over z, core).
Axes of the slice: x: 4, y: 4, z: 8, core: 2. Of those that a mesh axis runs over, the one named last changes fastest.
Arguments:
- ratings: bfloat16 [32768, 8192], P('users', 'items')
- observed: int32 [32768, 8192], P('users', 'items'), may hold values 0 or 1
- pool_profiles: bfloat16 [24576, 8192], P('users', 'items')
- neighbours: int32 [64, 2], P('users'), may hold values from 0 to 63, as said below
- test_matrix: bfloat16 [32768, 256], P('users'), may hold values from -6 to 6
Outputs:
- imputed: bfloat16 [32768, 8192], P('users', 'items')
- sketch: float32 [256, 8192], P('users', 'items')
The draws below stay inside these ranges and needn't reach their ends.
Inputs may be any that keep to these rules, and one draw needn't show every extreme that they name: `neighbours`: the 2 blocks of one query block are held by different indices of users; all query blocks of one index of users together name at most 1 block held by any one index of users, and exactly 1 from some.
All inputs are finite; a program needn't handle non-finite values. No bound on the sum of `observed` on one device may be relied on, other than what follows from the above.
Results may differ from the reference program's by a relative error of at most 0.0041.
Values may be sent and summed in bfloat16 or wider, within the bound.
A program may use at most 128 MiB of HBM per device.

```python
import math
import jax
import jax.numpy as jnp
from jax import lax

ITEMS = 8192
K = 256
QBLK = 512
QB_DEV = 4
NB = 2
PBLK = 384
PB_DEV = 4
QUSERS = 32768
QBLOCKS = 64
POOL = 24576
POOL_BLOCKS = 64


def profile(key, row_total):
    key_noise, key_spread, key_rows = jax.random.split(key, 3)
    level = 0.5 + jnp.arange(ITEMS, dtype=jnp.float32) / ITEMS
    spread = jnp.exp(jax.random.uniform(key_spread, (1, ITEMS), jnp.float32, math.log(0.3), math.log(3.0)))
    noise = jax.random.truncated_normal(key_noise, -4.0, 4.0, (row_total, ITEMS), jnp.float32)
    row_scale = jnp.exp(jax.random.uniform(key_rows, (row_total, 1), jnp.float32, math.log(0.3), math.log(3.0)))
    return (row_scale * (level[None, :] + spread * noise)).astype(jnp.bfloat16)


def draw_ratings(key, part):
    return profile(jax.random.fold_in(key, 11), QUSERS)


def draw_pool_profiles(key, part):
    return profile(jax.random.fold_in(key, 23), POOL)


def draw_neighbours(key, part):
    device_total = QBLOCKS // QB_DEV
    owner_total = POOL_BLOCKS // PB_DEV
    request_total = QB_DEV * NB
    repeats = max(1, request_total // owner_total)

    def one_device(device_key, device_index):
        key_owner, key_local = jax.random.split(device_key)
        shuffled = jax.random.permutation(key_owner, owner_total).astype(jnp.int32)
        rising = jnp.arange(owner_total, dtype=jnp.int32)
        falling = owner_total - 1 - rising
        order = jnp.where(device_index == 0, rising, jnp.where(device_index == 1, falling, shuffled))
        owners = jnp.tile(order, repeats)[:request_total]
        local_ids = jax.random.randint(key_local, (request_total,), 0, PB_DEV, dtype=jnp.int32)
        first_fixed = (device_index == 0) & (owners == 0)
        last_fixed = (device_index == 1) & (owners == owner_total - 1)
        local_ids = jnp.where(first_fixed, 0, jnp.where(last_fixed, PB_DEV - 1, local_ids)).astype(jnp.int32)
        return (owners * PB_DEV + local_ids).reshape(QB_DEV, NB)
    device_keys = jax.random.split(jax.random.fold_in(key, 37), device_total)
    device_ids = jnp.arange(device_total, dtype=jnp.int32)
    return jax.vmap(one_device)(device_keys, device_ids).reshape(QBLOCKS, NB).astype(jnp.int32)


def plant(values, rng, least, largest):
    longest = values.shape.index(max(values.shape))
    spots = []
    for shift in (0, 1):
        where = [jax.random.randint(jax.random.fold_in(rng, axis), (), 0, length) for axis, length in enumerate(values.shape)]
        where[longest] = (where[longest] + shift) % values.shape[longest]
        spots.append(tuple(where))
    return values.at[spots[0]].set(least).at[spots[1]].set(largest)


def level_of(key, shape, pieces, least, high):
    gain, own = 1.0, jax.random.fold_in(key, 6)
    for axis_at, shards_of in pieces:
        draws = jnp.exp(jax.random.uniform(jax.random.fold_in(own, axis_at), (shards_of,), jnp.float32, least / len(pieces), high / len(pieces)))
        gain = gain * jnp.repeat(draws, shape[axis_at] // shards_of).reshape([-1 if axis == axis_at else 1 for axis in range(len(shape))])
    return gain


def centred(stream_key, dims, scale, reach, pieces=(), kind=jnp.bfloat16):
    entries = jax.random.normal(stream_key, dims, jnp.float32) * scale
    if len(pieces) > 0:
        entries = level_of(stream_key, dims, pieces, -0.22, 0.18) * entries
    return jnp.clip(entries, min=-reach, max=reach).astype(kind)


def setup_inputs(seed: int = 0) -> dict:
    key_of = jax.random.split(jax.random.key(seed), 6)
    return {
        "ratings": draw_ratings(jax.random.fold_in(key_of[5], 71), 0),
        "observed": plant((jax.random.randint(key_of[1], (QUSERS, ITEMS), 0, 4) < 1).astype(jnp.int32), jax.random.fold_in(key_of[1], 1), 0, 1),
        "pool_profiles": draw_pool_profiles(jax.random.fold_in(key_of[5], 71), 0),
        "neighbours": draw_neighbours(jax.random.fold_in(key_of[5], 71), 0),
        "test_matrix": centred(key_of[4], (QUSERS, K), 1.0, 6.0, ((0, 16),)),
    }


def impute_block(block_args, pool_blocks, mean_blocks, scale_blocks):
    block_ratings, block_seen, query_mean, chosen = block_args
    seen_float = block_seen.astype(jnp.float32)
    rated = block_ratings.astype(jnp.float32)
    centered = (seen_float * (rated - query_mean[:, None])).astype(jnp.bfloat16)
    near_rows = jnp.take(pool_blocks, chosen, axis=0).reshape(NB * PBLK, ITEMS)
    near_mean = jnp.take(mean_blocks, chosen, axis=0).reshape(NB * PBLK)
    near_scale = jnp.take(scale_blocks, chosen, axis=0).reshape(NB * PBLK).astype(jnp.float32)
    raw_dots = lax.dot_general(centered, near_rows, (((1,), (1,)), ((), ())), preferred_element_type=jnp.float32)
    similar = raw_dots * near_scale[None, :]
    weights = (similar * lax.rsqrt(lax.optimization_barrier(jnp.sum(similar * similar, axis=1, keepdims=True)) + 1e-06)).astype(jnp.bfloat16)
    shift_term = jnp.dot(weights, near_rows, preferred_element_type=jnp.float32)
    shift_term = shift_term - jnp.dot(weights, near_mean, preferred_element_type=jnp.float32)[:, None]
    filled = query_mean[:, None] + shift_term
    return jnp.where(block_seen > 0, rated, filled).astype(jnp.bfloat16)

def reference(ratings, observed, pool_profiles, neighbours, test_matrix):
    seen_float = observed.astype(jnp.float32)
    query_sum = lax.optimization_barrier(jnp.sum(seen_float * ratings.astype(jnp.float32), axis=1))
    query_mean = query_sum / (lax.optimization_barrier(jnp.sum(seen_float, axis=1)) + 1.0)
    pool_float = pool_profiles.astype(jnp.float32)
    pool_mean = lax.optimization_barrier(jnp.mean(pool_float, axis=1))
    pool_var = lax.optimization_barrier(jnp.mean(jnp.square(pool_float - pool_mean[:, None]), axis=1))
    mean_half = pool_mean.astype(jnp.bfloat16)
    scale_half = lax.rsqrt(pool_var + 1e-05).astype(jnp.bfloat16)
    pool_blocks = pool_profiles.reshape(POOL_BLOCKS, PBLK, ITEMS)
    mean_blocks = mean_half.reshape(POOL_BLOCKS, PBLK)
    scale_blocks = scale_half.reshape(POOL_BLOCKS, PBLK)
    stacked = (ratings.reshape(QBLOCKS, QBLK, ITEMS), observed.reshape(QBLOCKS, QBLK, ITEMS), query_mean.reshape(QBLOCKS, QBLK), neighbours)
    imputed = lax.map(lambda block_args: impute_block(block_args, pool_blocks, mean_blocks, scale_blocks), stacked)
    imputed = imputed.reshape(QUSERS, ITEMS)
    sketch = lax.dot_general(test_matrix, imputed, (((0,), (0,)), ((), ())), preferred_element_type=jnp.float32)
    sketch = sketch * (1.0 / math.sqrt(QUSERS))
    return (imputed, sketch)
```

```python
import functools
import math

import jax
import jax.numpy as jnp
from jax import lax
from jax.experimental import pallas as pl
from jax.experimental.pallas import tpu as pltpu
from jax.sharding import PartitionSpec as P

MESH = pl.DeviceIdType.MESH
BF16 = jnp.bfloat16
F32 = jnp.float32

SIDE = 4
USERS = SIDE * SIDE
CHIPS = 8
PLUS = CHIPS // 2
MINUS = CHIPS - 1 - PLUS
ITEM_DEVS = 2 * CHIPS
QB = 4
QBLK = 512
PB = 4
PBLK = 384
NB = 2
NEAR = NB * PBLK
REQ = QB * NB
COLS = 512
KS = 256
HALF = QBLK // 2
CHUNK = HALF // CHIPS
ROWS = QB * QBLK
PROWS = PB * PBLK
PR = PBLK // SIDE
PC = COLS // SIDE
ITEMS = COLS * ITEM_DEVS
LAG = 5

ORDER = [
    (2, 2), (3, 2), (2, 3), (1, 2), (2, 1), (0, 2), (2, 0), (3, 1),
    (1, 3), (3, 3), (1, 1), (0, 3), (3, 0), (0, 1), (1, 0),
]


def nt(a, b):
    return lax.dot_general(a, b, (((1,), (1,)), ((), ())), preferred_element_type=F32)


def row_sums(x):
    ones = jnp.ones((8, 128), F32)
    return lax.dot_general(
        ones, x, (((1,), (1,)), ((), ())), precision=lax.Precision.HIGHEST, preferred_element_type=F32
    )[0:1]


def fold(x):
    return (x[:, 0:128] + x[:, 128:256]) + (x[:, 256:384] + x[:, 384:512])


def kernel(
    rat, obs, pool, nbr, test, imp, sketch,
    rat_v, obs_v, pool_v, test_v, nb_v, nb_s, spread, send2, near, cent, qm,
    st_own, st_in, ms_own, ms_all, sib_out, sib_in, own,
    up_out, up_in, dn_out, dn_in, wts, imp_v, sk, sk_in,
    ld, nb_ss, nb_rs, s1_ss, s1_rs, s2_ss, s2_rs, st_ss, st_rs, ms_ss, ms_rs,
    sib_ss, sib_rs, up_ss, up_rs, dn_ss, dn_rs, au_ss, au_rs, ad_ss, ad_rs,
    ax_ss, ax_rs, sk_ss, sk_rs, out_s,
):
    u = lax.axis_index("users")
    it = lax.axis_index("items")
    ux, uy = u // SIDE, u % SIDE
    z, c = it // 2, it % 2
    sent = []

    def user_at(dx, dy):
        return ((ux + dx) % SIDE) * SIDE + (uy + dy) % SIDE

    def chip_at(dz):
        return (u, ((z + dz + CHIPS) % CHIPS) * 2 + c)

    sibling = (u, z * 2 + (1 - c))

    def send(src, dst, ss, rs, dev):
        copy = pltpu.make_async_remote_copy(
            src_ref=src, dst_ref=dst, send_sem=ss, recv_sem=rs, device_id=dev, device_id_type=MESH
        )
        copy.start()
        sent.append(copy)

    def arrived(dst, ss, rs):
        pltpu.make_async_remote_copy(
            src_ref=dst, dst_ref=dst, send_sem=ss, recv_sem=rs, device_id=sibling, device_id_type=MESH
        ).wait_recv()

    def flush():
        for copy in sent:
            copy.wait_send()
        sent.clear()

    loads = [
        pltpu.make_async_copy(pool, pool_v, ld.at[0]),
        pltpu.make_async_copy(rat, rat_v, ld.at[1]),
        pltpu.make_async_copy(obs, obs_v, ld.at[2]),
        pltpu.make_async_copy(test, test_v, ld.at[3]),
        pltpu.make_async_copy(nbr, nb_v.at[u], ld.at[4]),
        pltpu.make_async_copy(
            pool.at[:, pl.ds(ux * PR, PR), pl.ds(pl.multiple_of(uy * PC, PC), PC)],
            spread.at[pl.ds(u * PB, PB)],
            ld.at[5],
        ),
    ]
    for load in loads:
        load.start()

    barrier = pltpu.get_barrier_semaphore()
    for dx, dy in ORDER:
        pl.semaphore_signal(barrier, inc=1, device_id=(user_at(dx, dy), it), device_id_type=MESH)
    for k in range(1, ITEM_DEVS):
        pl.semaphore_signal(
            barrier, inc=1, device_id=(u, (it + k) % ITEM_DEVS), device_id_type=MESH
        )
    pl.semaphore_wait(barrier, USERS - 1 + ITEM_DEVS - 1)

    for o, (dx, dy) in enumerate(ORDER):
        t = user_at(dx, dy)
        send(nbr, nb_v.at[u], nb_ss.at[o], nb_rs.at[o], (t, it))
    for o, (dx, dy) in enumerate(ORDER):
        t = user_at(dx, dy)
        send(
            pool.at[:, pl.ds((t // SIDE) * PR, PR), pl.ds(pl.multiple_of((t % SIDE) * PC, PC), PC)],
            spread.at[pl.ds(u * PB, PB)],
            s1_ss.at[o], s1_rs.at[o], (t, it),
        )

    loads[0].wait()
    for b in range(PB):
        p = pool_v[b].astype(F32)
        part = fold(p)
        mean = jnp.sum(part, axis=1, keepdims=True) * (1.0 / COLS)
        dev = p - mean
        st_own[2:3, b * PBLK:(b + 1) * PBLK] = row_sums(part)
        st_own[3:4, b * PBLK:(b + 1) * PBLK] = row_sums(fold(dev * dev))
    st_own[2:4, PROWS:ROWS] = jnp.zeros((2, ROWS - PROWS), F32)
    loads[1].wait()
    loads[2].wait()
    ones = jnp.ones((8, COLS), BF16)
    for b in range(ROWS // 256):
        rows = slice(b * 256, (b + 1) * 256)
        seen = obs_v[rows].astype(F32)
        masked = (seen * rat_v[rows].astype(F32)).astype(BF16)
        st_own[0:1, rows] = nt(ones, masked)[0:1]
        st_own[1:2, rows] = nt(ones, seen.astype(BF16))[0:1]
    for k in range(1, ITEM_DEVS):
        send(
            st_own, st_in.at[it], st_ss.at[k - 1], st_rs.at[k - 1],
            (u, (it + k) % ITEM_DEVS),
        )
    st_in[it] = st_own[...]

    loads[4].wait()
    for o, (dx, dy) in enumerate(ORDER):
        arrived(nb_v.at[user_at(-dx + SIDE, -dy + SIDE)], nb_ss.at[o], nb_rs.at[o])
    lists = pltpu.make_async_copy(nb_v, nb_s, ld.at[6])
    lists.start()
    lists.wait()
    loads[5].wait()
    for o, (dx, dy) in enumerate(ORDER):
        src = user_at(-dx + SIDE, -dy + SIDE)
        arrived(spread.at[pl.ds(src * PB, PB)], s1_ss.at[o], s1_rs.at[o])

    def deliver(b):
        for o, (dx, dy) in enumerate(ORDER):
            t = user_at(dx, dy)
            for k in range(b * NB, (b + 1) * NB):
                send2[o, k] = spread[nb_s[t, 0, k]]
            send(
                send2.at[o, pl.ds(b * NB, NB)],
                near.at[pl.ds(b * NB, NB), pl.ds(ux * PR, PR), pl.ds(pl.multiple_of(uy * PC, PC), PC)],
                s2_ss.at[b, o], s2_rs.at[b, o], (t, it),
            )
        for k in range(b * NB, (b + 1) * NB):
            near[k, pl.ds(pl.multiple_of(ux * PR, PR), PR), pl.ds(pl.multiple_of(uy * PC, PC), PC)] = spread[
                nb_s[u, 0, k]
            ]

    def delivered(b):
        for o, (dx, dy) in enumerate(ORDER):
            src = user_at(-dx + SIDE, -dy + SIDE)
            arrived(
                near.at[
                    pl.ds(b * NB, NB),
                    pl.ds((src // SIDE) * PR, PR),
                    pl.ds(pl.multiple_of((src % SIDE) * PC, PC), PC),
                ],
                s2_ss.at[b, o], s2_rs.at[b, o],
            )

    deliver(0)
    deliver(1)

    for k in range(1, ITEM_DEVS):
        src = (it + ITEM_DEVS - k) % ITEM_DEVS
        arrived(st_in.at[src], st_ss.at[k - 1], st_rs.at[k - 1])
    sums = st_in[0]
    for k in range(1, ITEM_DEVS):
        sums = sums + st_in[k]
    pool_mean = sums[2:3, 0:PROWS] * (1.0 / ITEMS)
    squares = sums[3:4, 0:PROWS]
    for k in range(ITEM_DEVS):
        gap = st_in[k, 2:3, 0:PROWS] * (1.0 / COLS) - pool_mean
        squares = squares + COLS * (gap * gap)
    scale = lax.rsqrt(squares * (1.0 / ITEMS) + 1e-05)
    blank = jnp.zeros((2, 128), F32)
    for b in range(PB):
        tiles = []
        for v in (pool_mean, scale):
            for j in range(PBLK // 128):
                at = b * PBLK + j * 128
                tiles.append(v[0:1, at:at + 128])
        tile = jnp.concatenate(tiles + [blank], axis=0)
        ms_own[b // 2, (b % 2) * 8:(b % 2) * 8 + 8] = tile
    ms_all[pl.ds(u * (PB // 2), PB // 2)] = ms_own[...].astype(BF16)
    for o, (dx, dy) in enumerate(ORDER):
        mine = ms_all.at[pl.ds(u * (PB // 2), PB // 2)]
        send(mine, mine, ms_ss.at[o], ms_rs.at[o], (user_at(dx, dy), it))
    deliver(2)
    deliver(3)

    def spread_mean(k, carry):
        at = pl.multiple_of(k * 128, 128)
        row = st_own[0:1, pl.ds(at, 128)]
        wide = jnp.broadcast_to(row, (128, 128)).T
        qm[pl.ds(at, 128)] = wide
        mean = jnp.concatenate([wide] * (COLS // 128), axis=1)
        seen = obs_v[pl.ds(at, 128)].astype(F32)
        cent[pl.ds(at, 128)] = (seen * (rat_v[pl.ds(at, 128)].astype(F32) - mean)).astype(BF16)
        return carry

    for copy in sent[2 * (USERS - 1):2 * (USERS - 1) + ITEM_DEVS - 1]:
        copy.wait_send()
    del sent[2 * (USERS - 1):2 * (USERS - 1) + ITEM_DEVS - 1]
    st_own[0:1] = sums[0:1] / (sums[1:2] + 1.0)
    lax.fori_loop(0, ROWS // 128, spread_mean, 0)
    for o, (dx, dy) in enumerate(ORDER):
        src = user_at(-dx + SIDE, -dy + SIDE)
        arrived(ms_all.at[pl.ds(src * (PB // 2), PB // 2)], ms_ss.at[o], ms_rs.at[o])
    loads[3].wait()

    up, down = chip_at(1), chip_at(-1)
    mine_at = c * HALF

    def stats_of(b):
        means, scales = [], []
        for k in range(b * NB, (b + 1) * NB):
            n = nb_s[u, 0, k]
            pair = ms_all[n // 2].astype(F32)
            tile = jnp.where(n % 2 == 0, pair[0:8], pair[8:16])
            means += [tile[j:j + 1] for j in range(3)]
            scales += [tile[j:j + 1] for j in range(3, 6)]
        return jnp.concatenate(means, axis=1), jnp.concatenate(scales, axis=1)

    def fill(b, at):
        w = wts[b, pl.ds(at, HALF)]
        pools = near[b * NB:(b + 1) * NB].reshape(NEAR, COLS)
        mean_row, _ = stats_of(b)
        mean_mat = jnp.broadcast_to(mean_row, (128, NEAR)).astype(BF16)
        shift = jnp.dot(w, pools, preferred_element_type=F32)
        rows = pl.ds(b * QBLK + at, HALF)
        base = qm[rows] - nt(w, mean_mat)
        filled = jnp.concatenate([base] * (COLS // 128), axis=1) + shift
        imp_v[rows] = jnp.where(obs_v[rows] > 0, rat_v[rows].astype(F32), filled).astype(BF16)

    def block(b):
        yield
        delivered(b)
        pools = near[b * NB:(b + 1) * NB].reshape(NEAR, COLS)
        theirs = pl.multiple_of(b * QBLK + (1 - c) * HALF, HALF)
        sib_out[b] = nt(cent[pl.ds(theirs, HALF)], pools).astype(BF16)
        send(sib_out.at[b], sib_in.at[b], sib_ss.at[b], sib_rs.at[b], sibling)
        mine = pl.multiple_of(b * QBLK + mine_at, HALF)
        own[b] = nt(cent[pl.ds(mine, HALF)], pools)
        yield
        arrived(sib_in.at[b], sib_ss.at[b], sib_rs.at[b])
        own[b] = own[b] + sib_in[b].astype(F32)

        def chunk(d):
            return own[b, pl.ds(pl.multiple_of(((z + d + CHIPS) % CHIPS) * CHUNK, CHUNK), CHUNK)]

        for s in range(PLUS):
            value = chunk(PLUS - s)
            if s > 0:
                arrived(up_in.at[b, s - 1], up_ss.at[b, s - 1], up_rs.at[b, s - 1])
                value = value + up_in[b, s - 1].astype(F32)
            up_out[b, s] = value.astype(BF16)
            send(up_out.at[b, s], up_in.at[b, s], up_ss.at[b, s], up_rs.at[b, s], up)
            if s < MINUS:
                value = chunk(s - MINUS)
                if s > 0:
                    arrived(dn_in.at[b, s - 1], dn_ss.at[b, s - 1], dn_rs.at[b, s - 1])
                    value = value + dn_in[b, s - 1].astype(F32)
                dn_out[b, s] = value.astype(BF16)
                send(dn_out.at[b, s], dn_in.at[b, s], dn_ss.at[b, s], dn_rs.at[b, s], down)
            yield
        s = PLUS - 1
        arrived(up_in.at[b, s], up_ss.at[b, s], up_rs.at[b, s])
        s = MINUS - 1
        arrived(dn_in.at[b, s], dn_ss.at[b, s], dn_rs.at[b, s])
        total = chunk(0) + (up_in[b, PLUS - 1].astype(F32) + dn_in[b, MINUS - 1].astype(F32))
        _, scale_row = stats_of(b)
        similar = total * scale_row
        norm = lax.rsqrt(jnp.sum(similar * similar, axis=1, keepdims=True) + 1e-06)

        def place(d, core):
            at = pl.multiple_of(core * HALF + ((z + d + CHIPS) % CHIPS) * CHUNK, CHUNK)
            return wts.at[b, pl.ds(at, CHUNK)]

        at = pl.multiple_of(mine_at + z * CHUNK, CHUNK)
        wts[b, pl.ds(at, CHUNK)] = (similar * norm).astype(BF16)

        def share(d, j):
            send(place(d, c), place(d, c), ax_ss.at[b, j], ax_rs.at[b, j], sibling)

        for s in range(PLUS):
            if s > 0:
                arrived(place(-s, c), au_ss.at[b, s - 1], au_rs.at[b, s - 1])
            send(place(-s, c), place(-s, c), au_ss.at[b, s], au_rs.at[b, s], up)
            if s < MINUS:
                if s > 0:
                    arrived(place(s, c), ad_ss.at[b, s - 1], ad_rs.at[b, s - 1])
                send(place(s, c), place(s, c), ad_ss.at[b, s], ad_rs.at[b, s], down)
                share(s, s)
            if s > 0:
                share(-s, MINUS + s)
            yield
        arrived(place(MINUS, c), ad_ss.at[b, MINUS - 1], ad_rs.at[b, MINUS - 1])
        share(MINUS, MINUS)
        arrived(place(-PLUS, c), au_ss.at[b, PLUS - 1], au_rs.at[b, PLUS - 1])
        share(-PLUS, MINUS + PLUS)
        fill(b, pl.multiple_of(mine_at, HALF))
        yield
        for d in range(MINUS + 1):
            arrived(place(d, 1 - c), ax_ss.at[b, d], ax_rs.at[b, d])
        for s in range(1, PLUS + 1):
            arrived(place(-s, 1 - c), ax_ss.at[b, MINUS + s], ax_rs.at[b, MINUS + s])
        fill(b, pl.multiple_of((1 - c) * HALF, HALF))
        rows = slice(b * QBLK, (b + 1) * QBLK)
        pltpu.make_async_copy(imp_v.at[rows], imp.at[rows], out_s.at[b]).start()
        part = lax.dot_general(
            test_v[rows], imp_v[rows], (((0,), (0,)), ((), ())), preferred_element_type=F32
        ).reshape(USERS, KS // USERS, COLS)
        sk[...] = part if b == 0 else sk[...] + part

    runs = [block(b) for b in range(QB)]
    live = list(range(QB))
    tick = 0
    while live:
        for b in list(live):
            if tick >= b * LAG and next(runs[b], "end") == "end":
                live.remove(b)
        tick += 1

    for o, (dx, dy) in enumerate(ORDER):
        t = user_at(dx, dy)
        send(sk.at[t], sk_in.at[u], sk_ss.at[o], sk_rs.at[o], (t, it))
    sk_in[u] = sk[u]
    for copy in sent[:-(USERS - 1)]:
        copy.wait_send()
    del sent[:-(USERS - 1)]
    for b in range(QB):
        rows = slice(b * QBLK, (b + 1) * QBLK)
        pltpu.make_async_copy(imp_v.at[rows], imp.at[rows], out_s.at[b]).wait()
    for o, (dx, dy) in enumerate(ORDER):
        arrived(sk_in.at[user_at(-dx + SIDE, -dy + SIDE)], sk_ss.at[o], sk_rs.at[o])
    total = sk_in[0]
    for k in range(1, USERS):
        total = total + sk_in[k]
    sketch[...] = total * (1.0 / math.sqrt(ROWS * USERS))
    flush()


def body(ratings, observed, pool_profiles, neighbours, test_matrix):
    lists = jnp.pad(neighbours.reshape(1, REQ), ((0, 7), (0, 128 - REQ)))
    pool = pool_profiles.reshape(PB, PBLK, COLS)
    dma = pltpu.SemaphoreType.DMA
    n = USERS - 1
    scratch = [
        pltpu.VMEM((ROWS, COLS), BF16),
        pltpu.VMEM((ROWS, COLS), jnp.int32),
        pltpu.VMEM((PB, PBLK, COLS), BF16),
        pltpu.VMEM((ROWS, KS), BF16),
        pltpu.VMEM((USERS, 8, 128), jnp.int32),
        pltpu.SMEM((USERS, 8, 128), jnp.int32),
        pltpu.VMEM((USERS * PB, PR, PC), BF16),
        pltpu.VMEM((n, REQ, PR, PC), BF16),
        pltpu.VMEM((REQ, PBLK, COLS), BF16),
        pltpu.VMEM((ROWS, COLS), BF16),
        pltpu.VMEM((ROWS, 128), F32),
        pltpu.VMEM((4, ROWS), F32),
        pltpu.VMEM((ITEM_DEVS, 4, ROWS), F32),
        pltpu.VMEM((PB // 2, 16, 128), F32),
        pltpu.VMEM((USERS * PB // 2, 16, 128), BF16),
        pltpu.VMEM((QB, HALF, NEAR), BF16),
        pltpu.VMEM((QB, HALF, NEAR), BF16),
        pltpu.VMEM((QB, HALF, NEAR), F32),
        pltpu.VMEM((QB, PLUS, CHUNK, NEAR), BF16),
        pltpu.VMEM((QB, PLUS, CHUNK, NEAR), BF16),
        pltpu.VMEM((QB, MINUS, CHUNK, NEAR), BF16),
        pltpu.VMEM((QB, MINUS, CHUNK, NEAR), BF16),
        pltpu.VMEM((QB, QBLK, NEAR), BF16),
        pltpu.VMEM((ROWS, COLS), BF16),
        pltpu.VMEM((USERS, KS // USERS, COLS), F32),
        pltpu.VMEM((USERS, KS // USERS, COLS), F32),
        dma((7,)),
    ]
    for shape in ((n,), (n,), (QB, n), (ITEM_DEVS - 1,), (n,), (QB,), (QB, PLUS), (QB, MINUS),
                  (QB, PLUS), (QB, MINUS), (QB, CHIPS), (n,)):
        scratch += [dma(shape), dma(shape)]
    scratch.append(dma((QB,)))
    hbm = pl.BlockSpec(memory_space=pl.ANY)
    vmem = pl.BlockSpec(memory_space=pltpu.VMEM)
    return pl.pallas_call(
        kernel,
        out_shape=(
            jax.ShapeDtypeStruct((ROWS, COLS), BF16),
            jax.ShapeDtypeStruct((KS // USERS, COLS), F32),
        ),
        in_specs=[hbm, hbm, hbm, vmem, hbm],
        out_specs=(hbm, vmem),
        scratch_shapes=scratch,
        compiler_params=pltpu.CompilerParams(
            collective_id=0, has_side_effects=True, vmem_limit_bytes=56 * 2**20
        ),
        name="impute_and_sketch",
    )(ratings, observed, pool, lists, test_matrix)


def solution(mesh):
    in_specs = (
        P("users", "items"),
        P("users", "items"),
        P("users", "items"),
        P("users", None),
        P("users", None),
    )
    out_specs = (P("users", "items"), P("users", "items"))
    return jax.shard_map(body, mesh=mesh, in_specs=in_specs, out_specs=out_specs, check_vma=False)
```

```python
import functools
import math

import jax
import jax.numpy as jnp
from jax import lax
from jax.experimental import pallas as pl
from jax.experimental.pallas import tpu as pltpu
from jax.sharding import PartitionSpec as P

MESH = pl.DeviceIdType.MESH
BF16 = jnp.bfloat16
F32 = jnp.float32

SIDE = 4
USERS = SIDE * SIDE
CHIPS = 8
PLUS = CHIPS // 2
MINUS = CHIPS - 1 - PLUS
ITEM_DEVS = 2 * CHIPS
QB = 4
QBLK = 512
PB = 4
PBLK = 384
NB = 2
NEAR = NB * PBLK
REQ = QB * NB
COLS = 512
KS = 256
HALF = QBLK // 2
CHUNK = HALF // CHIPS
ROWS = QB * QBLK
PROWS = PB * PBLK
PR = PBLK // SIDE
PC = COLS // SIDE
ITEMS = COLS * ITEM_DEVS
LAG = 1

ORDER = [
    (2, 2), (3, 2), (2, 3), (1, 2), (2, 1), (0, 2), (2, 0), (3, 1),
    (1, 3), (3, 3), (1, 1), (0, 3), (3, 0), (0, 1), (1, 0),
]


def nt(a, b):
    return lax.dot_general(a, b, (((1,), (1,)), ((), ())), preferred_element_type=F32)


def row_sums(x):
    ones = jnp.ones((8, 128), F32)
    return lax.dot_general(
        ones, x, (((1,), (1,)), ((), ())), precision=lax.Precision.HIGHEST, preferred_element_type=F32
    )[0:1]


def fold(x):
    return (x[:, 0:128] + x[:, 128:256]) + (x[:, 256:384] + x[:, 384:512])


def kernel(
    rat, obs, pool, nbr, test, imp, sketch,
    rat_v, obs_v, pool_v, test_v, nb_v, nb_s, spread, send2, near, cent, qm,
    st_own, st_in, st_sib, st_qm, ms_own, ms_all, sib_out, sib_in, own,
    up_out, up_in, dn_out, dn_in, wts, sk, sk_out, sk_in,
    ld, nb_ss, nb_rs, s1_ss, s1_rs, s2_ss, s2_rs, su_ss, su_rs, sd_ss, sd_rs, sx_ss, sx_rs, ms_ss, ms_rs,
    sib_ss, sib_rs, up_ss, up_rs, dn_ss, dn_rs, au_ss, au_rs, ad_ss, ad_rs,
    ax_ss, ax_rs, sk_ss, sk_rs,
):
    u = lax.axis_index("users")
    it = lax.axis_index("items")
    ux, uy = u // SIDE, u % SIDE
    z, c = it // 2, it % 2
    sent = []

    def user_at(dx, dy):
        return ((ux + dx) % SIDE) * SIDE + (uy + dy) % SIDE

    def chip_at(dz):
        return (u, ((z + dz + CHIPS) % CHIPS) * 2 + c)

    sibling = (u, z * 2 + (1 - c))
    up, down = chip_at(1), chip_at(-1)

    def send(src, dst, ss, rs, dev):
        copy = pltpu.make_async_remote_copy(
            src_ref=src, dst_ref=dst, send_sem=ss, recv_sem=rs, device_id=dev, device_id_type=MESH
        )
        copy.start()
        sent.append(copy)

    def arrived(dst, ss, rs):
        pltpu.make_async_remote_copy(
            src_ref=dst, dst_ref=dst, send_sem=ss, recv_sem=rs, device_id=sibling, device_id_type=MESH
        ).wait_recv()

    def flush():
        for copy in sent:
            copy.wait_send()
        sent.clear()

    loads = [
        pltpu.make_async_copy(pool, pool_v, ld.at[0]),
        pltpu.make_async_copy(rat, rat_v, ld.at[1]),
        pltpu.make_async_copy(obs, obs_v, ld.at[2]),
        pltpu.make_async_copy(test, test_v, ld.at[3]),
        pltpu.make_async_copy(nbr, nb_v.at[u], ld.at[4]),
        pltpu.make_async_copy(
            pool.at[:, pl.ds(ux * PR, PR), pl.ds(pl.multiple_of(uy * PC, PC), PC)],
            spread.at[pl.ds(u * PB, PB)],
            ld.at[5],
        ),
    ]
    for load in loads:
        load.start()

    barrier = pltpu.get_barrier_semaphore()
    for dx, dy in ORDER:
        pl.semaphore_signal(barrier, inc=1, device_id=(user_at(dx, dy), it), device_id_type=MESH)
    for neighbour in (sibling, up, down):
        pl.semaphore_signal(barrier, inc=1, device_id=neighbour, device_id_type=MESH)
    pl.semaphore_wait(barrier, USERS - 1 + 3)

    for o, (dx, dy) in enumerate(ORDER):
        t = user_at(dx, dy)
        send(nbr, nb_v.at[u], nb_ss.at[o], nb_rs.at[o], (t, it))
    for o, (dx, dy) in enumerate(ORDER):
        t = user_at(dx, dy)
        send(
            pool.at[:, pl.ds((t // SIDE) * PR, PR), pl.ds(pl.multiple_of((t % SIDE) * PC, PC), PC)],
            spread.at[pl.ds(u * PB, PB)],
            s1_ss.at[o], s1_rs.at[o], (t, it),
        )

    loads[0].wait()
    for b in range(PB):
        p = pool_v[b].astype(F32)
        part = fold(p)
        mean = jnp.sum(part, axis=1, keepdims=True) * (1.0 / COLS)
        dev = p - mean
        st_own[2:3, b * PBLK:(b + 1) * PBLK] = row_sums(part)
        st_own[3:4, b * PBLK:(b + 1) * PBLK] = row_sums(fold(dev * dev))
    st_own[2:4, PROWS:ROWS] = jnp.zeros((2, ROWS - PROWS), F32)
    loads[1].wait()
    loads[2].wait()
    ones = jnp.ones((8, COLS), BF16)
    for b in range(ROWS // 256):
        rows = slice(b * 256, (b + 1) * 256)
        seen = obs_v[rows].astype(F32)
        masked = (seen * rat_v[rows].astype(F32)).astype(BF16)
        st_own[0:1, rows] = nt(ones, masked)[0:1]
        st_own[1:2, rows] = nt(ones, seen.astype(BF16))[0:1]
    st_in[z] = st_own[...]

    def stats_from(d):
        return st_in.at[(z + d + CHIPS) % CHIPS]

    for s in range(PLUS):
        if s > 0:
            arrived(stats_from(-s), su_ss.at[s - 1], su_rs.at[s - 1])
        send(stats_from(-s), stats_from(-s), su_ss.at[s], su_rs.at[s], up)
        if s < MINUS:
            if s > 0:
                arrived(stats_from(s), sd_ss.at[s - 1], sd_rs.at[s - 1])
            send(stats_from(s), stats_from(s), sd_ss.at[s], sd_rs.at[s], down)
    arrived(stats_from(-PLUS), su_ss.at[PLUS - 1], su_rs.at[PLUS - 1])
    arrived(stats_from(MINUS), sd_ss.at[MINUS - 1], sd_rs.at[MINUS - 1])

    sums = st_in[0]
    for k in range(1, CHIPS):
        sums = sums + st_in[k]
    core_mean = sums[2:3, 0:PROWS] * (1.0 / (CHIPS * COLS))
    squares = sums[3:4, 0:PROWS]
    for k in range(CHIPS):
        gap = st_in[k, 2:3, 0:PROWS] * (1.0 / COLS) - core_mean
        squares = squares + COLS * (gap * gap)
    st_own[0:2] = sums[0:2]
    st_own[2:3, 0:PROWS] = core_mean
    st_own[3:4, 0:PROWS] = squares
    send(st_own, st_sib, sx_ss.at[0], sx_rs.at[0], sibling)

    loads[4].wait()
    for o, (dx, dy) in enumerate(ORDER):
        arrived(nb_v.at[user_at(-dx + SIDE, -dy + SIDE)], nb_ss.at[o], nb_rs.at[o])
    lists = pltpu.make_async_copy(nb_v, nb_s, ld.at[6])
    lists.start()
    lists.wait()
    loads[5].wait()
    for o, (dx, dy) in enumerate(ORDER):
        src = user_at(-dx + SIDE, -dy + SIDE)
        arrived(spread.at[pl.ds(src * PB, PB)], s1_ss.at[o], s1_rs.at[o])

    def deliver(b):
        for o, (dx, dy) in enumerate(ORDER):
            t = user_at(dx, dy)
            for k in range(b * NB, (b + 1) * NB):
                send2[o, k] = spread[nb_s[t, k // NB, k % NB]]
            send(
                send2.at[o, pl.ds(b * NB, NB)],
                near.at[pl.ds(b * NB, NB), pl.ds(ux * PR, PR), pl.ds(pl.multiple_of(uy * PC, PC), PC)],
                s2_ss.at[b, o], s2_rs.at[b, o], (t, it),
            )
        for k in range(b * NB, (b + 1) * NB):
            near[k, pl.ds(pl.multiple_of(ux * PR, PR), PR), pl.ds(pl.multiple_of(uy * PC, PC), PC)] = spread[
                nb_s[u, k // NB, k % NB]
            ]

    def delivered(b):
        for o, (dx, dy) in enumerate(ORDER):
            src = user_at(-dx + SIDE, -dy + SIDE)
            arrived(
                near.at[
                    pl.ds(b * NB, NB),
                    pl.ds((src // SIDE) * PR, PR),
                    pl.ds(pl.multiple_of((src % SIDE) * PC, PC), PC),
                ],
                s2_ss.at[b, o], s2_rs.at[b, o],
            )

    deliver(0)
    deliver(1)

    arrived(st_sib, sx_ss.at[0], sx_rs.at[0])
    core_mean, other_mean = st_own[2:3, 0:PROWS], st_sib[2:3, 0:PROWS]
    pool_mean = (core_mean + other_mean) * 0.5
    gap = core_mean - other_mean
    squares = (st_own[3:4, 0:PROWS] + st_sib[3:4, 0:PROWS]) + (CHIPS * COLS * 0.5) * (gap * gap)
    scale = lax.rsqrt(squares * (1.0 / ITEMS) + 1e-05)
    blank = jnp.zeros((2, 128), F32)
    for b in range(PB):
        tiles = []
        for v in (pool_mean, scale):
            for j in range(PBLK // 128):
                at = b * PBLK + j * 128
                tiles.append(v[0:1, at:at + 128])
        tile = jnp.concatenate(tiles + [blank], axis=0)
        ms_own[b // 2, (b % 2) * 8:(b % 2) * 8 + 8] = tile
    ms_all[pl.ds(u * (PB // 2), PB // 2)] = ms_own[...].astype(BF16)
    for o, (dx, dy) in enumerate(ORDER):
        mine = ms_all.at[pl.ds(u * (PB // 2), PB // 2)]
        send(mine, mine, ms_ss.at[o], ms_rs.at[o], (user_at(dx, dy), it))
    deliver(2)
    deliver(3)

    def spread_mean(k, carry):
        at = pl.multiple_of(k * 128, 128)
        row = st_qm[0:1, pl.ds(at, 128)]
        wide = jnp.broadcast_to(row, (128, 128)).T
        qm[pl.ds(at, 128)] = wide
        mean = jnp.concatenate([wide] * (COLS // 128), axis=1)
        seen = obs_v[pl.ds(at, 128)].astype(F32)
        cent[pl.ds(at, 128)] = (seen * (rat_v[pl.ds(at, 128)].astype(F32) - mean)).astype(BF16)
        return carry

    st_qm[...] = (st_own[0:1] + st_sib[0:1]) / (st_own[1:2] + st_sib[1:2] + 1.0)
    lax.fori_loop(0, ROWS // 128, spread_mean, 0)
    for o, (dx, dy) in enumerate(ORDER):
        src = user_at(-dx + SIDE, -dy + SIDE)
        arrived(ms_all.at[pl.ds(src * (PB // 2), PB // 2)], ms_ss.at[o], ms_rs.at[o])
    loads[3].wait()

    mine_at = c * HALF

    def stats_of(b):
        means, scales = [], []
        for k in range(b * NB, (b + 1) * NB):
            n = nb_s[u, k // NB, k % NB]
            pair = ms_all[n // 2].astype(F32)
            tile = jnp.where(n % 2 == 0, pair[0:8], pair[8:16])
            means += [tile[j:j + 1] for j in range(3)]
            scales += [tile[j:j + 1] for j in range(3, 6)]
        return jnp.concatenate(means, axis=1), jnp.concatenate(scales, axis=1)

    def fill(b, at):
        w = wts[b, pl.ds(at, HALF)]
        pools = near[b * NB:(b + 1) * NB].reshape(NEAR, COLS)
        mean_row, _ = stats_of(b)
        mean_mat = jnp.broadcast_to(mean_row, (128, NEAR)).astype(BF16)
        shift = jnp.dot(w, pools, preferred_element_type=F32)
        rows = pl.ds(b * QBLK + at, HALF)
        base = qm[rows] - nt(w, mean_mat)
        filled = jnp.concatenate([base] * (COLS // 128), axis=1) + shift
        imp[rows] = jnp.where(obs_v[rows] > 0, rat_v[rows].astype(F32), filled).astype(BF16)

    def block(b):
        yield
        delivered(b)
        pools = near[b * NB:(b + 1) * NB].reshape(NEAR, COLS)
        theirs = pl.multiple_of(b * QBLK + (1 - c) * HALF, HALF)
        sib_out[b] = nt(cent[pl.ds(theirs, HALF)], pools).astype(BF16)
        send(sib_out.at[b], sib_in.at[b], sib_ss.at[b], sib_rs.at[b], sibling)
        mine = pl.multiple_of(b * QBLK + mine_at, HALF)
        own[b] = nt(cent[pl.ds(mine, HALF)], pools)
        yield
        arrived(sib_in.at[b], sib_ss.at[b], sib_rs.at[b])
        own[b] = own[b] + sib_in[b].astype(F32)

        def chunk(d):
            return own[b, pl.ds(pl.multiple_of(((z + d + CHIPS) % CHIPS) * CHUNK, CHUNK), CHUNK)]

        for s in range(PLUS):
            value = chunk(PLUS - s)
            if s > 0:
                arrived(up_in.at[b, s - 1], up_ss.at[b, s - 1], up_rs.at[b, s - 1])
                value = value + up_in[b, s - 1].astype(F32)
            up_out[b, s] = value.astype(BF16)
            send(up_out.at[b, s], up_in.at[b, s], up_ss.at[b, s], up_rs.at[b, s], up)
            if s < MINUS:
                value = chunk(s - MINUS)
                if s > 0:
                    arrived(dn_in.at[b, s - 1], dn_ss.at[b, s - 1], dn_rs.at[b, s - 1])
                    value = value + dn_in[b, s - 1].astype(F32)
                dn_out[b, s] = value.astype(BF16)
                send(dn_out.at[b, s], dn_in.at[b, s], dn_ss.at[b, s], dn_rs.at[b, s], down)
            yield
        s = PLUS - 1
        arrived(up_in.at[b, s], up_ss.at[b, s], up_rs.at[b, s])
        s = MINUS - 1
        arrived(dn_in.at[b, s], dn_ss.at[b, s], dn_rs.at[b, s])
        total = chunk(0) + (up_in[b, PLUS - 1].astype(F32) + dn_in[b, MINUS - 1].astype(F32))
        _, scale_row = stats_of(b)
        similar = total * scale_row
        norm = lax.rsqrt(jnp.sum(similar * similar, axis=1, keepdims=True) + 1e-06)

        def place(d, core):
            at = pl.multiple_of(core * HALF + ((z + d + CHIPS) % CHIPS) * CHUNK, CHUNK)
            return wts.at[b, pl.ds(at, CHUNK)]

        at = pl.multiple_of(mine_at + z * CHUNK, CHUNK)
        wts[b, pl.ds(at, CHUNK)] = (similar * norm).astype(BF16)

        def share(d, j):
            send(place(d, c), place(d, c), ax_ss.at[b, j], ax_rs.at[b, j], sibling)

        for s in range(PLUS):
            if s > 0:
                arrived(place(-s, c), au_ss.at[b, s - 1], au_rs.at[b, s - 1])
            send(place(-s, c), place(-s, c), au_ss.at[b, s], au_rs.at[b, s], up)
            if s < MINUS:
                if s > 0:
                    arrived(place(s, c), ad_ss.at[b, s - 1], ad_rs.at[b, s - 1])
                send(place(s, c), place(s, c), ad_ss.at[b, s], ad_rs.at[b, s], down)
                share(s, s)
            if s > 0:
                share(-s, MINUS + s)
            yield
        arrived(place(MINUS, c), ad_ss.at[b, MINUS - 1], ad_rs.at[b, MINUS - 1])
        share(MINUS, MINUS)
        arrived(place(-PLUS, c), au_ss.at[b, PLUS - 1], au_rs.at[b, PLUS - 1])
        share(-PLUS, MINUS + PLUS)
        fill(b, pl.multiple_of(mine_at, HALF))
        yield
        for d in range(MINUS + 1):
            arrived(place(d, 1 - c), ax_ss.at[b, d], ax_rs.at[b, d])
        for s in range(1, PLUS + 1):
            arrived(place(-s, 1 - c), ax_ss.at[b, MINUS + s], ax_rs.at[b, MINUS + s])
        fill(b, pl.multiple_of((1 - c) * HALF, HALF))
        rows = slice(b * QBLK, (b + 1) * QBLK)
        part = lax.dot_general(
            test_v[rows], imp[rows], (((0,), (0,)), ((), ())), preferred_element_type=F32
        ).reshape(USERS, KS // USERS, COLS)
        sk[...] = part if b == 0 else sk[...] + part

    runs = [block(b) for b in range(QB)]
    live = list(range(QB))
    tick = 0
    while live:
        for b in list(live):
            if tick >= b * LAG and next(runs[b], "end") == "end":
                live.remove(b)
        tick += 1

    sk_out[...] = sk[...].astype(BF16)
    for o, (dx, dy) in enumerate(ORDER):
        t = user_at(dx, dy)
        send(sk_out.at[t], sk_in.at[u], sk_ss.at[o], sk_rs.at[o], (t, it))
    for copy in sent[:-(USERS - 1)]:
        copy.wait_send()
    del sent[:-(USERS - 1)]
    for o, (dx, dy) in enumerate(ORDER):
        arrived(sk_in.at[user_at(-dx + SIDE, -dy + SIDE)], sk_ss.at[o], sk_rs.at[o])
    total = sk[u]
    for dx, dy in ORDER:
        total = total + sk_in[user_at(dx, dy)].astype(F32)
    sketch[...] = total * (1.0 / math.sqrt(ROWS * USERS))
    flush()


def body(ratings, observed, pool_profiles, neighbours, test_matrix):
    pool = pool_profiles.reshape(PB, PBLK, COLS)
    dma = pltpu.SemaphoreType.DMA
    n = USERS - 1
    scratch = [
        pltpu.VMEM((ROWS, COLS), BF16),
        pltpu.VMEM((ROWS, COLS), jnp.int32),
        pltpu.VMEM((PB, PBLK, COLS), BF16),
        pltpu.VMEM((ROWS, KS), BF16),
        pltpu.VMEM((USERS, QB, NB), jnp.int32),
        pltpu.SMEM((USERS, QB, NB), jnp.int32),
        pltpu.VMEM((USERS * PB, PR, PC), BF16),
        pltpu.VMEM((n, REQ, PR, PC), BF16),
        pltpu.VMEM((REQ, PBLK, COLS), BF16),
        pltpu.VMEM((ROWS, COLS), BF16),
        pltpu.VMEM((ROWS, 128), F32),
        pltpu.VMEM((4, ROWS), F32),
        pltpu.VMEM((CHIPS, 4, ROWS), F32),
        pltpu.VMEM((4, ROWS), F32),
        pltpu.VMEM((1, ROWS), F32),
        pltpu.VMEM((PB // 2, 16, 128), F32),
        pltpu.VMEM((USERS * PB // 2, 16, 128), BF16),
        pltpu.VMEM((QB, HALF, NEAR), BF16),
        pltpu.VMEM((QB, HALF, NEAR), BF16),
        pltpu.VMEM((QB, HALF, NEAR), F32),
        pltpu.VMEM((QB, PLUS, CHUNK, NEAR), BF16),
        pltpu.VMEM((QB, PLUS, CHUNK, NEAR), BF16),
        pltpu.VMEM((QB, MINUS, CHUNK, NEAR), BF16),
        pltpu.VMEM((QB, MINUS, CHUNK, NEAR), BF16),
        pltpu.VMEM((QB, QBLK, NEAR), BF16),
        pltpu.VMEM((USERS, KS // USERS, COLS), F32),
        pltpu.VMEM((USERS, KS // USERS, COLS), BF16),
        pltpu.VMEM((USERS, KS // USERS, COLS), BF16),
        dma((7,)),
    ]
    for shape in ((n,), (n,), (QB, n), (PLUS,), (MINUS,), (1,), (n,), (QB,), (QB, PLUS), (QB, MINUS),
                  (QB, PLUS), (QB, MINUS), (QB, CHIPS), (n,)):
        scratch += [dma(shape), dma(shape)]
    hbm = pl.BlockSpec(memory_space=pl.ANY)
    vmem = pl.BlockSpec(memory_space=pltpu.VMEM)
    return pl.pallas_call(
        kernel,
        out_shape=(
            pltpu.VMEM((ROWS, COLS), BF16),
            pltpu.VMEM((KS // USERS, COLS), F32),
        ),
        in_specs=[hbm, hbm, hbm, vmem, hbm],
        out_specs=(vmem, vmem),
        scratch_shapes=scratch,
        compiler_params=pltpu.CompilerParams(
            collective_id=0, has_side_effects=True, vmem_limit_bytes=58 * 2**20
        ),
        name="impute_and_sketch",
    )(ratings, observed, pool, neighbours, test_matrix)


def solution(mesh):
    in_specs = (
        P("users", "items"),
        P("users", "items"),
        P("users", "items"),
        P("users", None),
        P("users", None),
    )
    out_specs = (P("users", "items"), P("users", "items"))
    return jax.shard_map(body, mesh=mesh, in_specs=in_specs, out_specs=out_specs, check_vma=False)
```

```python
import functools
import math

import jax
import jax.numpy as jnp
from jax import lax
from jax.experimental import pallas as pl
from jax.experimental.pallas import tpu as pltpu
from jax.sharding import PartitionSpec as P

MESH = pl.DeviceIdType.MESH
BF16 = jnp.bfloat16
F32 = jnp.float32

SIDE = 4
USERS = SIDE * SIDE
CHIPS = 8
PLUS = CHIPS // 2
MINUS = CHIPS - 1 - PLUS
ITEM_DEVS = 2 * CHIPS
QB = 4
QBLK = 512
PB = 4
PBLK = 384
NB = 2
NEAR = NB * PBLK
REQ = QB * NB
COLS = 512
KS = 256
HALF = QBLK // 2
CHUNK = HALF // CHIPS
ROWS = QB * QBLK
PROWS = PB * PBLK
PR = PBLK // SIDE
PC = COLS // SIDE
ITEMS = COLS * ITEM_DEVS
LAG = 1

ORDER = [
    (2, 2), (1, 0), (0, 1), (2, 1), (0, 3), (3, 0), (1, 2), (2, 3),
    (3, 2), (1, 1), (3, 3), (2, 0), (0, 2), (1, 3), (3, 1),
]


def nt(a, b):
    return lax.dot_general(a, b, (((1,), (1,)), ((), ())), preferred_element_type=F32)


def row_sums(x):
    ones = jnp.ones((8, 128), F32)
    return lax.dot_general(
        ones, x, (((1,), (1,)), ((), ())), precision=lax.Precision.HIGHEST, preferred_element_type=F32
    )[0:1]


def fold(x):
    return (x[:, 0:128] + x[:, 128:256]) + (x[:, 256:384] + x[:, 384:512])


def kernel(
    rat, obs, pool, nbr, test, imp, sketch,
    rat_v, obs_v, pool_v, test_v, nb_v, nb_s, spread, send2, near, cent, qm,
    st_own, st_in, st_sib, st_qm, ms_own, ms_all, sib_out, sib_in, own,
    up_out, up_in, dn_out, dn_in, wts, sk, sk_out, sk_in,
    ld, nb_ss, nb_rs, s1_ss, s1_rs, s2_ss, s2_rs, su_ss, su_rs, sd_ss, sd_rs, sx_ss, sx_rs, ms_ss, ms_rs,
    sib_ss, sib_rs, up_ss, up_rs, dn_ss, dn_rs, au_ss, au_rs, ad_ss, ad_rs,
    ax_ss, ax_rs, sk_ss, sk_rs,
):
    u = lax.axis_index("users")
    it = lax.axis_index("items")
    ux, uy = u // SIDE, u % SIDE
    z, c = it // 2, it % 2
    sent = []

    def user_at(dx, dy):
        return ((ux + dx) % SIDE) * SIDE + (uy + dy) % SIDE

    def chip_at(dz):
        return (u, ((z + dz + CHIPS) % CHIPS) * 2 + c)

    sibling = (u, z * 2 + (1 - c))
    up, down = chip_at(1), chip_at(-1)

    def send(src, dst, ss, rs, dev):
        copy = pltpu.make_async_remote_copy(
            src_ref=src, dst_ref=dst, send_sem=ss, recv_sem=rs, device_id=dev, device_id_type=MESH
        )
        copy.start()
        sent.append(copy)

    def arrived(dst, ss, rs):
        pltpu.make_async_remote_copy(
            src_ref=dst, dst_ref=dst, send_sem=ss, recv_sem=rs, device_id=sibling, device_id_type=MESH
        ).wait_recv()

    def flush():
        for copy in sent:
            copy.wait_send()
        sent.clear()

    loads = [
        pltpu.make_async_copy(pool, pool_v, ld.at[0]),
        pltpu.make_async_copy(rat, rat_v, ld.at[1]),
        pltpu.make_async_copy(obs, obs_v, ld.at[2]),
        pltpu.make_async_copy(test, test_v, ld.at[3]),
        pltpu.make_async_copy(nbr, nb_v.at[u], ld.at[4]),
        pltpu.make_async_copy(
            pool.at[:, pl.ds(ux * PR, PR), pl.ds(pl.multiple_of(uy * PC, PC), PC)],
            spread.at[pl.ds(u * PB, PB)],
            ld.at[5],
        ),
    ]
    for load in loads:
        load.start()

    barrier = pltpu.get_barrier_semaphore()
    for dx, dy in ORDER:
        pl.semaphore_signal(barrier, inc=1, device_id=(user_at(dx, dy), it), device_id_type=MESH)
    for neighbour in (sibling, up, down):
        pl.semaphore_signal(barrier, inc=1, device_id=neighbour, device_id_type=MESH)
    pl.semaphore_wait(barrier, USERS - 1 + 3)

    for o, (dx, dy) in enumerate(ORDER):
        t = user_at(dx, dy)
        send(nbr, nb_v.at[u], nb_ss.at[o], nb_rs.at[o], (t, it))
    for o, (dx, dy) in enumerate(ORDER):
        t = user_at(dx, dy)
        send(
            pool.at[:, pl.ds((t // SIDE) * PR, PR), pl.ds(pl.multiple_of((t % SIDE) * PC, PC), PC)],
            spread.at[pl.ds(u * PB, PB)],
            s1_ss.at[o], s1_rs.at[o], (t, it),
        )

    loads[0].wait()
    for b in range(PB):
        p = pool_v[b].astype(F32)
        part = fold(p)
        mean = jnp.sum(part, axis=1, keepdims=True) * (1.0 / COLS)
        dev = p - mean
        st_own[2:3, b * PBLK:(b + 1) * PBLK] = row_sums(part)
        st_own[3:4, b * PBLK:(b + 1) * PBLK] = row_sums(fold(dev * dev))
    st_own[2:4, PROWS:ROWS] = jnp.zeros((2, ROWS - PROWS), F32)
    loads[1].wait()
    loads[2].wait()
    ones = jnp.ones((8, COLS), BF16)
    for b in range(ROWS // 256):
        rows = slice(b * 256, (b + 1) * 256)
        seen = obs_v[rows].astype(F32)
        masked = (seen * rat_v[rows].astype(F32)).astype(BF16)
        st_own[0:1, rows] = nt(ones, masked)[0:1]
        st_own[1:2, rows] = nt(ones, seen.astype(BF16))[0:1]
    st_in[z] = st_own[...]

    def stats_from(d):
        return st_in.at[(z + d + CHIPS) % CHIPS]

    for s in range(PLUS):
        if s > 0:
            arrived(stats_from(-s), su_ss.at[s - 1], su_rs.at[s - 1])
        send(stats_from(-s), stats_from(-s), su_ss.at[s], su_rs.at[s], up)
        if s < MINUS:
            if s > 0:
                arrived(stats_from(s), sd_ss.at[s - 1], sd_rs.at[s - 1])
            send(stats_from(s), stats_from(s), sd_ss.at[s], sd_rs.at[s], down)
    arrived(stats_from(-PLUS), su_ss.at[PLUS - 1], su_rs.at[PLUS - 1])
    arrived(stats_from(MINUS), sd_ss.at[MINUS - 1], sd_rs.at[MINUS - 1])

    sums = st_in[0]
    for k in range(1, CHIPS):
        sums = sums + st_in[k]
    core_mean = sums[2:3, 0:PROWS] * (1.0 / (CHIPS * COLS))
    squares = sums[3:4, 0:PROWS]
    for k in range(CHIPS):
        gap = st_in[k, 2:3, 0:PROWS] * (1.0 / COLS) - core_mean
        squares = squares + COLS * (gap * gap)
    st_own[0:2] = sums[0:2]
    st_own[2:3, 0:PROWS] = core_mean
    st_own[3:4, 0:PROWS] = squares
    send(st_own, st_sib, sx_ss.at[0], sx_rs.at[0], sibling)

    loads[4].wait()
    for o, (dx, dy) in enumerate(ORDER):
        arrived(nb_v.at[user_at(-dx + SIDE, -dy + SIDE)], nb_ss.at[o], nb_rs.at[o])
    lists = pltpu.make_async_copy(nb_v, nb_s, ld.at[6])
    lists.start()
    lists.wait()
    loads[5].wait()
    for o, (dx, dy) in enumerate(ORDER):
        src = user_at(-dx + SIDE, -dy + SIDE)
        arrived(spread.at[pl.ds(src * PB, PB)], s1_ss.at[o], s1_rs.at[o])

    def deliver(b):
        for o, (dx, dy) in enumerate(ORDER):
            t = user_at(dx, dy)
            for k in range(b * NB, (b + 1) * NB):
                send2[o, k] = spread[nb_s[t, k % NB, k // NB]]
            send(
                send2.at[o, pl.ds(b * NB, NB)],
                near.at[pl.ds(b * NB, NB), pl.ds(ux * PR, PR), pl.ds(pl.multiple_of(uy * PC, PC), PC)],
                s2_ss.at[b, o], s2_rs.at[b, o], (t, it),
            )
        for k in range(b * NB, (b + 1) * NB):
            near[k, pl.ds(pl.multiple_of(ux * PR, PR), PR), pl.ds(pl.multiple_of(uy * PC, PC), PC)] = spread[
                nb_s[u, k % NB, k // NB]
            ]

    def delivered(b):
        for o, (dx, dy) in enumerate(ORDER):
            src = user_at(-dx + SIDE, -dy + SIDE)
            arrived(
                near.at[
                    pl.ds(b * NB, NB),
                    pl.ds((src // SIDE) * PR, PR),
                    pl.ds(pl.multiple_of((src % SIDE) * PC, PC), PC),
                ],
                s2_ss.at[b, o], s2_rs.at[b, o],
            )

    deliver(0)
    deliver(1)

    arrived(st_sib, sx_ss.at[0], sx_rs.at[0])
    core_mean, other_mean = st_own[2:3, 0:PROWS], st_sib[2:3, 0:PROWS]
    pool_mean = (core_mean + other_mean) * 0.5
    gap = core_mean - other_mean
    squares = (st_own[3:4, 0:PROWS] + st_sib[3:4, 0:PROWS]) + (CHIPS * COLS * 0.5) * (gap * gap)
    scale = lax.rsqrt(squares * (1.0 / ITEMS) + 1e-05)
    blank = jnp.zeros((2, 128), F32)
    for b in range(PB):
        tiles = []
        for v in (pool_mean, scale):
            for j in range(PBLK // 128):
                at = b * PBLK + j * 128
                tiles.append(v[0:1, at:at + 128])
        tile = jnp.concatenate(tiles + [blank], axis=0)
        ms_own[b // 2, (b % 2) * 8:(b % 2) * 8 + 8] = tile
    ms_all[pl.ds(u * (PB // 2), PB // 2)] = ms_own[...].astype(BF16)
    for o, (dx, dy) in enumerate(ORDER):
        mine = ms_all.at[pl.ds(u * (PB // 2), PB // 2)]
        send(mine, mine, ms_ss.at[o], ms_rs.at[o], (user_at(dx, dy), it))
    deliver(2)
    deliver(3)

    def spread_mean(k, carry):
        at = pl.multiple_of(k * 128, 128)
        row = st_qm[0:1, pl.ds(at, 128)]
        wide = jnp.broadcast_to(row, (128, 128)).T
        qm[pl.ds(at, 128)] = wide
        mean = jnp.concatenate([wide] * (COLS // 128), axis=1)
        seen = obs_v[pl.ds(at, 128)].astype(F32)
        cent[pl.ds(at, 128)] = (seen * (rat_v[pl.ds(at, 128)].astype(F32) - mean)).astype(BF16)
        return carry

    st_qm[...] = (st_own[0:1] + st_sib[0:1]) / (st_own[1:2] + st_sib[1:2] + 1.0)
    lax.fori_loop(0, ROWS // 128, spread_mean, 0)
    for o, (dx, dy) in enumerate(ORDER):
        src = user_at(-dx + SIDE, -dy + SIDE)
        arrived(ms_all.at[pl.ds(src * (PB // 2), PB // 2)], ms_ss.at[o], ms_rs.at[o])
    loads[3].wait()

    mine_at = c * HALF

    def stats_of(b):
        means, scales = [], []
        for k in range(b * NB, (b + 1) * NB):
            n = nb_s[u, k % NB, k // NB]
            pair = ms_all[n // 2].astype(F32)
            tile = jnp.where(n % 2 == 0, pair[0:8], pair[8:16])
            means += [tile[j:j + 1] for j in range(3)]
            scales += [tile[j:j + 1] for j in range(3, 6)]
        return jnp.concatenate(means, axis=1), jnp.concatenate(scales, axis=1)

    def fill(b, at):
        w = wts[b, pl.ds(at, HALF)]
        pools = near[b * NB:(b + 1) * NB].reshape(NEAR, COLS)
        mean_row, _ = stats_of(b)
        mean_mat = jnp.broadcast_to(mean_row, (128, NEAR)).astype(BF16)
        shift = jnp.dot(w, pools, preferred_element_type=F32)
        rows = pl.ds(b * QBLK + at, HALF)
        base = qm[rows] - nt(w, mean_mat)
        filled = jnp.concatenate([base] * (COLS // 128), axis=1) + shift
        imp[rows] = jnp.where(obs_v[rows] > 0, rat_v[rows].astype(F32), filled).astype(BF16)

    def block(b):
        yield
        delivered(b)
        pools = near[b * NB:(b + 1) * NB].reshape(NEAR, COLS)
        theirs = pl.multiple_of(b * QBLK + (1 - c) * HALF, HALF)
        sib_out[b] = nt(cent[pl.ds(theirs, HALF)], pools).astype(BF16)
        send(sib_out.at[b], sib_in.at[b], sib_ss.at[b], sib_rs.at[b], sibling)
        mine = pl.multiple_of(b * QBLK + mine_at, HALF)
        own[b] = nt(cent[pl.ds(mine, HALF)], pools)
        yield
        arrived(sib_in.at[b], sib_ss.at[b], sib_rs.at[b])
        own[b] = own[b] + sib_in[b].astype(F32)

        def chunk(d):
            return own[b, pl.ds(pl.multiple_of(((z + d + CHIPS) % CHIPS) * CHUNK, CHUNK), CHUNK)]

        for s in range(PLUS):
            value = chunk(PLUS - s)
            if s > 0:
                arrived(up_in.at[b, s - 1], up_ss.at[b, s - 1], up_rs.at[b, s - 1])
                value = value + up_in[b, s - 1].astype(F32)
            up_out[b, s] = value.astype(BF16)
            send(up_out.at[b, s], up_in.at[b, s], up_ss.at[b, s], up_rs.at[b, s], up)
            if s < MINUS:
                value = chunk(s - MINUS)
                if s > 0:
                    arrived(dn_in.at[b, s - 1], dn_ss.at[b, s - 1], dn_rs.at[b, s - 1])
                    value = value + dn_in[b, s - 1].astype(F32)
                dn_out[b, s] = value.astype(BF16)
                send(dn_out.at[b, s], dn_in.at[b, s], dn_ss.at[b, s], dn_rs.at[b, s], down)
            yield
        s = PLUS - 1
        arrived(up_in.at[b, s], up_ss.at[b, s], up_rs.at[b, s])
        s = MINUS - 1
        arrived(dn_in.at[b, s], dn_ss.at[b, s], dn_rs.at[b, s])
        total = chunk(0) + (up_in[b, PLUS - 1].astype(F32) + dn_in[b, MINUS - 1].astype(F32))
        _, scale_row = stats_of(b)
        similar = total * scale_row
        norm = lax.rsqrt(jnp.sum(similar * similar, axis=1, keepdims=True) + 1e-06)

        def place(d, core):
            at = pl.multiple_of(core * HALF + ((z + d + CHIPS) % CHIPS) * CHUNK, CHUNK)
            return wts.at[b, pl.ds(at, CHUNK)]

        at = pl.multiple_of(mine_at + z * CHUNK, CHUNK)
        wts[b, pl.ds(at, CHUNK)] = (similar * norm).astype(BF16)

        def share(d, j):
            send(place(d, c), place(d, c), ax_ss.at[b, j], ax_rs.at[b, j], sibling)

        for s in range(PLUS):
            if s > 0:
                arrived(place(-s, c), au_ss.at[b, s - 1], au_rs.at[b, s - 1])
            send(place(-s, c), place(-s, c), au_ss.at[b, s], au_rs.at[b, s], up)
            if s < MINUS:
                if s > 0:
                    arrived(place(s, c), ad_ss.at[b, s - 1], ad_rs.at[b, s - 1])
                send(place(s, c), place(s, c), ad_ss.at[b, s], ad_rs.at[b, s], down)
                share(s, s)
            if s > 0:
                share(-s, MINUS + s)
            yield
        arrived(place(MINUS, c), ad_ss.at[b, MINUS - 1], ad_rs.at[b, MINUS - 1])
        share(MINUS, MINUS)
        arrived(place(-PLUS, c), au_ss.at[b, PLUS - 1], au_rs.at[b, PLUS - 1])
        share(-PLUS, MINUS + PLUS)
        fill(b, pl.multiple_of(mine_at, HALF))
        yield
        for d in range(MINUS + 1):
            arrived(place(d, 1 - c), ax_ss.at[b, d], ax_rs.at[b, d])
        for s in range(1, PLUS + 1):
            arrived(place(-s, 1 - c), ax_ss.at[b, MINUS + s], ax_rs.at[b, MINUS + s])
        fill(b, pl.multiple_of((1 - c) * HALF, HALF))
        rows = slice(b * QBLK, (b + 1) * QBLK)
        part = lax.dot_general(
            test_v[rows], imp[rows], (((0,), (0,)), ((), ())), preferred_element_type=F32
        ).reshape(USERS, KS // USERS, COLS)
        sk[...] = part if b == 0 else sk[...] + part

    runs = [block(b) for b in range(QB)]
    live = list(range(QB))
    tick = 0
    while live:
        for b in list(live):
            if tick >= b * LAG and next(runs[b], "end") == "end":
                live.remove(b)
        tick += 1

    sk_out[...] = sk[...].astype(BF16)
    for o, (dx, dy) in enumerate(ORDER):
        t = user_at(dx, dy)
        send(sk_out.at[t], sk_in.at[u], sk_ss.at[o], sk_rs.at[o], (t, it))
    for copy in sent[:-(USERS - 1)]:
        copy.wait_send()
    del sent[:-(USERS - 1)]
    for o, (dx, dy) in enumerate(ORDER):
        arrived(sk_in.at[user_at(-dx + SIDE, -dy + SIDE)], sk_ss.at[o], sk_rs.at[o])
    total = sk[u]
    for dx, dy in ORDER:
        total = total + sk_in[user_at(dx, dy)].astype(F32)
    sketch[...] = total * (1.0 / math.sqrt(ROWS * USERS))
    flush()


def body(ratings, observed, pool_profiles, neighbours, test_matrix):
    pool = pool_profiles.reshape(PB, PBLK, COLS)
    dma = pltpu.SemaphoreType.DMA
    n = USERS - 1
    scratch = [
        pltpu.VMEM((ROWS, COLS), BF16),
        pltpu.VMEM((ROWS, COLS), jnp.int32),
        pltpu.VMEM((PB, PBLK, COLS), BF16),
        pltpu.VMEM((ROWS, KS), BF16),
        pltpu.VMEM((USERS, NB, QB), jnp.int32),
        pltpu.SMEM((USERS, NB, QB), jnp.int32),
        pltpu.VMEM((USERS * PB, PR, PC), BF16),
        pltpu.VMEM((n, REQ, PR, PC), BF16),
        pltpu.VMEM((REQ, PBLK, COLS), BF16),
        pltpu.VMEM((ROWS, COLS), BF16),
        pltpu.VMEM((ROWS, 128), F32),
        pltpu.VMEM((4, ROWS), F32),
        pltpu.VMEM((CHIPS, 4, ROWS), F32),
        pltpu.VMEM((4, ROWS), F32),
        pltpu.VMEM((1, ROWS), F32),
        pltpu.VMEM((PB // 2, 16, 128), F32),
        pltpu.VMEM((USERS * PB // 2, 16, 128), BF16),
        pltpu.VMEM((QB, HALF, NEAR), BF16),
        pltpu.VMEM((QB, HALF, NEAR), BF16),
        pltpu.VMEM((QB, HALF, NEAR), F32),
        pltpu.VMEM((QB, PLUS, CHUNK, NEAR), BF16),
        pltpu.VMEM((QB, PLUS, CHUNK, NEAR), BF16),
        pltpu.VMEM((QB, MINUS, CHUNK, NEAR), BF16),
        pltpu.VMEM((QB, MINUS, CHUNK, NEAR), BF16),
        pltpu.VMEM((QB, QBLK, NEAR), BF16),
        pltpu.VMEM((USERS, KS // USERS, COLS), F32),
        pltpu.VMEM((USERS, KS // USERS, COLS), BF16),
        pltpu.VMEM((USERS, KS // USERS, COLS), BF16),
        dma((7,)),
    ]
    for shape in ((n,), (n,), (QB, n), (PLUS,), (MINUS,), (1,), (n,), (QB,), (QB, PLUS), (QB, MINUS),
                  (QB, PLUS), (QB, MINUS), (QB, CHIPS), (n,)):
        scratch += [dma(shape), dma(shape)]
    hbm = pl.BlockSpec(memory_space=pl.ANY)
    vmem = pl.BlockSpec(memory_space=pltpu.VMEM)
    return pl.pallas_call(
        kernel,
        out_shape=(
            pltpu.VMEM((ROWS, COLS), BF16),
            pltpu.VMEM((KS // USERS, COLS), F32),
        ),
        in_specs=[hbm, hbm, hbm, hbm, hbm],
        out_specs=(vmem, vmem),
        scratch_shapes=scratch,
        compiler_params=pltpu.CompilerParams(
            collective_id=0, has_side_effects=True, vmem_limit_bytes=58 * 2**20
        ),
        name="impute_and_sketch",
    )(ratings, observed, pool, neighbours.T, test_matrix)


def solution(mesh):
    in_specs = (
        P("users", "items"),
        P("users", "items"),
        P("users", "items"),
        P("users", None),
        P("users", None),
    )
    out_specs = (P("users", "items"), P("users", "items"))
    return jax.shard_map(body, mesh=mesh, in_specs=in_specs, out_specs=out_specs, check_vma=False)
```

```python
import functools
import math

import jax
import jax.numpy as jnp
from jax import lax
from jax.experimental import pallas as pl
from jax.experimental.pallas import tpu as pltpu
from jax.sharding import PartitionSpec as P

MESH = pl.DeviceIdType.MESH
BF16 = jnp.bfloat16
F32 = jnp.float32

SIDE = 4
USERS = SIDE * SIDE
CHIPS = 8
PLUS = CHIPS // 2
MINUS = CHIPS - 1 - PLUS
ITEM_DEVS = 2 * CHIPS
QB = 4
QBLK = 512
PB = 4
PBLK = 384
NB = 2
NEAR = NB * PBLK
REQ = QB * NB
COLS = 512
KS = 256
HALF = QBLK // 2
CHUNK = HALF // CHIPS
ROWS = QB * QBLK
PROWS = PB * PBLK
PR = PBLK // SIDE
PC = COLS // SIDE
ITEMS = COLS * ITEM_DEVS
LAG = 1

ORDER = [
    (2, 2), (1, 0), (0, 1), (2, 1), (0, 3), (3, 0), (1, 2), (2, 3),
    (3, 2), (1, 1), (3, 3), (2, 0), (0, 2), (1, 3), (3, 1),
]


def nt(a, b):
    return lax.dot_general(a, b, (((1,), (1,)), ((), ())), preferred_element_type=F32)


def row_sums(x):
    ones = jnp.ones((8, 128), F32)
    return lax.dot_general(
        ones, x, (((1,), (1,)), ((), ())), precision=lax.Precision.HIGHEST, preferred_element_type=F32
    )[0:1]


def fold(x):
    return (x[:, 0:128] + x[:, 128:256]) + (x[:, 256:384] + x[:, 384:512])


def kernel(
    rat, obs, pool, nbr, test, imp, sketch,
    rat_v, obs_v, pool_v, test_v, nb_v, nb_s, spread, send2, near, cent, qm,
    st_own, st_in, st_sib, st_qm, ms_own, ms_all, sib_out, sib_in, own,
    up_out, up_in, dn_out, dn_in, wts, sk, sk_out, sk_in,
    ld, nb_ss, nb_rs, s1_ss, s1_rs, s2_ss, s2_rs, su_ss, su_rs, sd_ss, sd_rs, sx_ss, sx_rs, ms_ss, ms_rs,
    sib_ss, sib_rs, up_ss, up_rs, dn_ss, dn_rs, au_ss, au_rs, ad_ss, ad_rs,
    ax_ss, ax_rs, sk_ss, sk_rs,
):
    u = lax.axis_index("users")
    it = lax.axis_index("items")
    ux, uy = u // SIDE, u % SIDE
    z, c = it // 2, it % 2
    sent = []

    def user_at(dx, dy):
        return ((ux + dx) % SIDE) * SIDE + (uy + dy) % SIDE

    def chip_at(dz):
        return (u, ((z + dz + CHIPS) % CHIPS) * 2 + c)

    sibling = (u, z * 2 + (1 - c))
    up, down = chip_at(1), chip_at(-1)

    def send(src, dst, ss, rs, dev):
        copy = pltpu.make_async_remote_copy(
            src_ref=src, dst_ref=dst, send_sem=ss, recv_sem=rs, device_id=dev, device_id_type=MESH
        )
        copy.start()
        sent.append(copy)

    def arrived(dst, ss, rs):
        pltpu.make_async_remote_copy(
            src_ref=dst, dst_ref=dst, send_sem=ss, recv_sem=rs, device_id=sibling, device_id_type=MESH
        ).wait_recv()

    def flush():
        for copy in sent:
            copy.wait_send()
        sent.clear()

    loads = [
        pltpu.make_async_copy(pool, pool_v, ld.at[0]),
        pltpu.make_async_copy(rat, rat_v, ld.at[1]),
        pltpu.make_async_copy(obs, obs_v, ld.at[2]),
        pltpu.make_async_copy(test, test_v, ld.at[3]),
        pltpu.make_async_copy(nbr, nb_v.at[u], ld.at[4]),
        pltpu.make_async_copy(
            pool.at[:, pl.ds(ux * PR, PR), pl.ds(pl.multiple_of(uy * PC, PC), PC)],
            spread.at[pl.ds(u * PB, PB)],
            ld.at[5],
        ),
    ]
    for load in loads:
        load.start()

    barrier = pltpu.get_barrier_semaphore()
    for dx, dy in ORDER:
        pl.semaphore_signal(barrier, inc=1, device_id=(user_at(dx, dy), it), device_id_type=MESH)
    for neighbour in (sibling, up, down):
        pl.semaphore_signal(barrier, inc=1, device_id=neighbour, device_id_type=MESH)
    pl.semaphore_wait(barrier, USERS - 1 + 3)

    for o, (dx, dy) in enumerate(ORDER):
        t = user_at(dx, dy)
        send(nbr, nb_v.at[u], nb_ss.at[o], nb_rs.at[o], (t, it))
    for o, (dx, dy) in enumerate(ORDER):
        t = user_at(dx, dy)
        send(
            pool.at[:, pl.ds((t // SIDE) * PR, PR), pl.ds(pl.multiple_of((t % SIDE) * PC, PC), PC)],
            spread.at[pl.ds(u * PB, PB)],
            s1_ss.at[o], s1_rs.at[o], (t, it),
        )

    loads[0].wait()
    for b in range(PB):
        p = pool_v[b].astype(F32)
        part = fold(p)
        mean = jnp.sum(part, axis=1, keepdims=True) * (1.0 / COLS)
        dev = p - mean
        st_own[2:3, b * PBLK:(b + 1) * PBLK] = row_sums(part)
        st_own[3:4, b * PBLK:(b + 1) * PBLK] = row_sums(fold(dev * dev))
    st_own[2:4, PROWS:ROWS] = jnp.zeros((2, ROWS - PROWS), F32)
    loads[1].wait()
    loads[2].wait()
    ones = jnp.ones((8, COLS), BF16)
    for b in range(ROWS // 256):
        rows = slice(b * 256, (b + 1) * 256)
        seen = obs_v[rows].astype(F32)
        masked = (seen * rat_v[rows].astype(F32)).astype(BF16)
        st_own[0:1, rows] = nt(ones, masked)[0:1]
        st_own[1:2, rows] = nt(ones, seen.astype(BF16))[0:1]
    st_in[z] = st_own[...]

    def stats_from(d):
        return st_in.at[(z + d + CHIPS) % CHIPS]

    for s in range(PLUS):
        if s > 0:
            arrived(stats_from(-s), su_ss.at[s - 1], su_rs.at[s - 1])
        send(stats_from(-s), stats_from(-s), su_ss.at[s], su_rs.at[s], up)
        if s < MINUS:
            if s > 0:
                arrived(stats_from(s), sd_ss.at[s - 1], sd_rs.at[s - 1])
            send(stats_from(s), stats_from(s), sd_ss.at[s], sd_rs.at[s], down)
    arrived(stats_from(-PLUS), su_ss.at[PLUS - 1], su_rs.at[PLUS - 1])
    arrived(stats_from(MINUS), sd_ss.at[MINUS - 1], sd_rs.at[MINUS - 1])

    sums = st_in[0]
    for k in range(1, CHIPS):
        sums = sums + st_in[k]
    core_mean = sums[2:3, 0:PROWS] * (1.0 / (CHIPS * COLS))
    squares = sums[3:4, 0:PROWS]
    for k in range(CHIPS):
        gap = st_in[k, 2:3, 0:PROWS] * (1.0 / COLS) - core_mean
        squares = squares + COLS * (gap * gap)
    st_own[0:2] = sums[0:2]
    st_own[2:3, 0:PROWS] = core_mean
    st_own[3:4, 0:PROWS] = squares
    send(st_own, st_sib, sx_ss.at[0], sx_rs.at[0], sibling)

    arrived(st_sib, sx_ss.at[0], sx_rs.at[0])
    core_mean, other_mean = st_own[2:3, 0:PROWS], st_sib[2:3, 0:PROWS]
    pool_mean = (core_mean + other_mean) * 0.5
    gap = core_mean - other_mean
    squares = (st_own[3:4, 0:PROWS] + st_sib[3:4, 0:PROWS]) + (CHIPS * COLS * 0.5) * (gap * gap)
    scale = lax.rsqrt(squares * (1.0 / ITEMS) + 1e-05)
    blank = jnp.zeros((2, 128), F32)
    for b in range(PB):
        tiles = []
        for v in (pool_mean, scale):
            for j in range(PBLK // 128):
                at = b * PBLK + j * 128
                tiles.append(v[0:1, at:at + 128])
        tile = jnp.concatenate(tiles + [blank], axis=0)
        ms_own[b // 2, (b % 2) * 8:(b % 2) * 8 + 8] = tile
    ms_all[pl.ds(u * (PB // 2), PB // 2)] = ms_own[...].astype(BF16)
    for o, (dx, dy) in enumerate(ORDER):
        mine = ms_all.at[pl.ds(u * (PB // 2), PB // 2)]
        send(mine, mine, ms_ss.at[o], ms_rs.at[o], (user_at(dx, dy), it))
    loads[4].wait()
    for o, (dx, dy) in enumerate(ORDER):
        arrived(nb_v.at[user_at(-dx + SIDE, -dy + SIDE)], nb_ss.at[o], nb_rs.at[o])
    lists = pltpu.make_async_copy(nb_v, nb_s, ld.at[6])
    lists.start()
    lists.wait()
    loads[5].wait()
    for o, (dx, dy) in enumerate(ORDER):
        src = user_at(-dx + SIDE, -dy + SIDE)
        arrived(spread.at[pl.ds(src * PB, PB)], s1_ss.at[o], s1_rs.at[o])

    def deliver(b):
        for o, (dx, dy) in enumerate(ORDER):
            t = user_at(dx, dy)
            for k in range(b * NB, (b + 1) * NB):
                send2[o, k] = spread[nb_s[t, k % NB, k // NB]]
            send(
                send2.at[o, pl.ds(b * NB, NB)],
                near.at[pl.ds(b * NB, NB), pl.ds(ux * PR, PR), pl.ds(pl.multiple_of(uy * PC, PC), PC)],
                s2_ss.at[b, o], s2_rs.at[b, o], (t, it),
            )
        for k in range(b * NB, (b + 1) * NB):
            near[k, pl.ds(pl.multiple_of(ux * PR, PR), PR), pl.ds(pl.multiple_of(uy * PC, PC), PC)] = spread[
                nb_s[u, k % NB, k // NB]
            ]

    def delivered(b):
        for o, (dx, dy) in enumerate(ORDER):
            src = user_at(-dx + SIDE, -dy + SIDE)
            arrived(
                near.at[
                    pl.ds(b * NB, NB),
                    pl.ds((src // SIDE) * PR, PR),
                    pl.ds(pl.multiple_of((src % SIDE) * PC, PC), PC),
                ],
                s2_ss.at[b, o], s2_rs.at[b, o],
            )

    deliver(0)
    deliver(1)

    deliver(2)
    deliver(3)

    def spread_mean(k, carry):
        at = pl.multiple_of(k * 128, 128)
        row = st_qm[0:1, pl.ds(at, 128)]
        wide = jnp.broadcast_to(row, (128, 128)).T
        qm[pl.ds(at, 128)] = wide
        mean = jnp.concatenate([wide] * (COLS // 128), axis=1)
        seen = obs_v[pl.ds(at, 128)].astype(F32)
        cent[pl.ds(at, 128)] = (seen * (rat_v[pl.ds(at, 128)].astype(F32) - mean)).astype(BF16)
        return carry

    st_qm[...] = (st_own[0:1] + st_sib[0:1]) / (st_own[1:2] + st_sib[1:2] + 1.0)
    lax.fori_loop(0, ROWS // 128, spread_mean, 0)
    for o, (dx, dy) in enumerate(ORDER):
        src = user_at(-dx + SIDE, -dy + SIDE)
        arrived(ms_all.at[pl.ds(src * (PB // 2), PB // 2)], ms_ss.at[o], ms_rs.at[o])
    loads[3].wait()

    mine_at = c * HALF

    def stats_of(b):
        means, scales = [], []
        for k in range(b * NB, (b + 1) * NB):
            n = nb_s[u, k % NB, k // NB]
            pair = ms_all[n // 2].astype(F32)
            tile = jnp.where(n % 2 == 0, pair[0:8], pair[8:16])
            means += [tile[j:j + 1] for j in range(3)]
            scales += [tile[j:j + 1] for j in range(3, 6)]
        return jnp.concatenate(means, axis=1), jnp.concatenate(scales, axis=1)

    def fill(b, at):
        w = wts[b, pl.ds(at, HALF)]
        pools = near[b * NB:(b + 1) * NB].reshape(NEAR, COLS)
        mean_row, _ = stats_of(b)
        mean_mat = jnp.broadcast_to(mean_row, (128, NEAR)).astype(BF16)
        shift = jnp.dot(w, pools, preferred_element_type=F32)
        rows = pl.ds(b * QBLK + at, HALF)
        base = qm[rows] - nt(w, mean_mat)
        filled = jnp.concatenate([base] * (COLS // 128), axis=1) + shift
        imp[rows] = jnp.where(obs_v[rows] > 0, rat_v[rows].astype(F32), filled).astype(BF16)

    def block(b):
        yield
        delivered(b)
        pools = near[b * NB:(b + 1) * NB].reshape(NEAR, COLS)
        theirs = pl.multiple_of(b * QBLK + (1 - c) * HALF, HALF)
        sib_out[b] = nt(cent[pl.ds(theirs, HALF)], pools).astype(BF16)
        send(sib_out.at[b], sib_in.at[b], sib_ss.at[b], sib_rs.at[b], sibling)
        mine = pl.multiple_of(b * QBLK + mine_at, HALF)
        own[b] = nt(cent[pl.ds(mine, HALF)], pools)
        yield
        arrived(sib_in.at[b], sib_ss.at[b], sib_rs.at[b])
        own[b] = own[b] + sib_in[b].astype(F32)

        def chunk(d):
            return own[b, pl.ds(pl.multiple_of(((z + d + CHIPS) % CHIPS) * CHUNK, CHUNK), CHUNK)]

        for s in range(PLUS):
            value = chunk(PLUS - s)
            if s > 0:
                arrived(up_in.at[b, s - 1], up_ss.at[b, s - 1], up_rs.at[b, s - 1])
                value = value + up_in[b, s - 1].astype(F32)
            up_out[b, s] = value.astype(BF16)
            send(up_out.at[b, s], up_in.at[b, s], up_ss.at[b, s], up_rs.at[b, s], up)
            if s < MINUS:
                value = chunk(s - MINUS)
                if s > 0:
                    arrived(dn_in.at[b, s - 1], dn_ss.at[b, s - 1], dn_rs.at[b, s - 1])
                    value = value + dn_in[b, s - 1].astype(F32)
                dn_out[b, s] = value.astype(BF16)
                send(dn_out.at[b, s], dn_in.at[b, s], dn_ss.at[b, s], dn_rs.at[b, s], down)
            yield
        s = PLUS - 1
        arrived(up_in.at[b, s], up_ss.at[b, s], up_rs.at[b, s])
        s = MINUS - 1
        arrived(dn_in.at[b, s], dn_ss.at[b, s], dn_rs.at[b, s])
        total = chunk(0) + (up_in[b, PLUS - 1].astype(F32) + dn_in[b, MINUS - 1].astype(F32))
        _, scale_row = stats_of(b)
        similar = total * scale_row
        norm = lax.rsqrt(jnp.sum(similar * similar, axis=1, keepdims=True) + 1e-06)

        def place(d, core):
            at = pl.multiple_of(core * HALF + ((z + d + CHIPS) % CHIPS) * CHUNK, CHUNK)
            return wts.at[b, pl.ds(at, CHUNK)]

        at = pl.multiple_of(mine_at + z * CHUNK, CHUNK)
        wts[b, pl.ds(at, CHUNK)] = (similar * norm).astype(BF16)

        def share(d, j):
            send(place(d, c), place(d, c), ax_ss.at[b, j], ax_rs.at[b, j], sibling)

        for s in range(PLUS):
            if s > 0:
                arrived(place(-s, c), au_ss.at[b, s - 1], au_rs.at[b, s - 1])
            send(place(-s, c), place(-s, c), au_ss.at[b, s], au_rs.at[b, s], up)
            if s < MINUS:
                if s > 0:
                    arrived(place(s, c), ad_ss.at[b, s - 1], ad_rs.at[b, s - 1])
                send(place(s, c), place(s, c), ad_ss.at[b, s], ad_rs.at[b, s], down)
                share(s, s)
            if s > 0:
                share(-s, MINUS + s)
            yield
        arrived(place(MINUS, c), ad_ss.at[b, MINUS - 1], ad_rs.at[b, MINUS - 1])
        share(MINUS, MINUS)
        arrived(place(-PLUS, c), au_ss.at[b, PLUS - 1], au_rs.at[b, PLUS - 1])
        share(-PLUS, MINUS + PLUS)
        fill(b, pl.multiple_of(mine_at, HALF))
        yield
        for d in range(MINUS + 1):
            arrived(place(d, 1 - c), ax_ss.at[b, d], ax_rs.at[b, d])
        for s in range(1, PLUS + 1):
            arrived(place(-s, 1 - c), ax_ss.at[b, MINUS + s], ax_rs.at[b, MINUS + s])
        fill(b, pl.multiple_of((1 - c) * HALF, HALF))
        rows = slice(b * QBLK, (b + 1) * QBLK)
        part = lax.dot_general(
            test_v[rows], imp[rows], (((0,), (0,)), ((), ())), preferred_element_type=F32
        ).reshape(USERS, KS // USERS, COLS)
        sk[...] = part if b == 0 else sk[...] + part

    runs = [block(b) for b in range(QB)]
    live = list(range(QB))
    tick = 0
    while live:
        for b in list(live):
            if tick >= b * LAG and next(runs[b], "end") == "end":
                live.remove(b)
        tick += 1

    sk_out[...] = sk[...].astype(BF16)
    for o, (dx, dy) in enumerate(ORDER):
        t = user_at(dx, dy)
        send(sk_out.at[t], sk_in.at[u], sk_ss.at[o], sk_rs.at[o], (t, it))
    for copy in sent[:-(USERS - 1)]:
        copy.wait_send()
    del sent[:-(USERS - 1)]
    for o, (dx, dy) in enumerate(ORDER):
        arrived(sk_in.at[user_at(-dx + SIDE, -dy + SIDE)], sk_ss.at[o], sk_rs.at[o])
    total = sk[u]
    for dx, dy in ORDER:
        total = total + sk_in[user_at(dx, dy)].astype(F32)
    sketch[...] = total * (1.0 / math.sqrt(ROWS * USERS))
    flush()


def body(ratings, observed, pool_profiles, neighbours, test_matrix):
    pool = pool_profiles.reshape(PB, PBLK, COLS)
    dma = pltpu.SemaphoreType.DMA
    n = USERS - 1
    scratch = [
        pltpu.VMEM((ROWS, COLS), BF16),
        pltpu.VMEM((ROWS, COLS), jnp.int32),
        pltpu.VMEM((PB, PBLK, COLS), BF16),
        pltpu.VMEM((ROWS, KS), BF16),
        pltpu.VMEM((USERS, NB, QB), jnp.int32),
        pltpu.SMEM((USERS, NB, QB), jnp.int32),
        pltpu.VMEM((USERS * PB, PR, PC), BF16),
        pltpu.VMEM((n, REQ, PR, PC), BF16),
        pltpu.VMEM((REQ, PBLK, COLS), BF16),
        pltpu.VMEM((ROWS, COLS), BF16),
        pltpu.VMEM((ROWS, 128), F32),
        pltpu.VMEM((4, ROWS), F32),
        pltpu.VMEM((CHIPS, 4, ROWS), F32),
        pltpu.VMEM((4, ROWS), F32),
        pltpu.VMEM((1, ROWS), F32),
        pltpu.VMEM((PB // 2, 16, 128), F32),
        pltpu.VMEM((USERS * PB // 2, 16, 128), BF16),
        pltpu.VMEM((QB, HALF, NEAR), BF16),
        pltpu.VMEM((QB, HALF, NEAR), BF16),
        pltpu.VMEM((QB, HALF, NEAR), F32),
        pltpu.VMEM((QB, PLUS, CHUNK, NEAR), BF16),
        pltpu.VMEM((QB, PLUS, CHUNK, NEAR), BF16),
        pltpu.VMEM((QB, MINUS, CHUNK, NEAR), BF16),
        pltpu.VMEM((QB, MINUS, CHUNK, NEAR), BF16),
        pltpu.VMEM((QB, QBLK, NEAR), BF16),
        pltpu.VMEM((USERS, KS // USERS, COLS), F32),
        pltpu.VMEM((USERS, KS // USERS, COLS), BF16),
        pltpu.VMEM((USERS, KS // USERS, COLS), BF16),
        dma((7,)),
    ]
    for shape in ((n,), (n,), (QB, n), (PLUS,), (MINUS,), (1,), (n,), (QB,), (QB, PLUS), (QB, MINUS),
                  (QB, PLUS), (QB, MINUS), (QB, CHIPS), (n,)):
        scratch += [dma(shape), dma(shape)]
    hbm = pl.BlockSpec(memory_space=pl.ANY)
    vmem = pl.BlockSpec(memory_space=pltpu.VMEM)
    return pl.pallas_call(
        kernel,
        out_shape=(
            pltpu.VMEM((ROWS, COLS), BF16),
            pltpu.VMEM((KS // USERS, COLS), F32),
        ),
        in_specs=[hbm, hbm, hbm, hbm, hbm],
        out_specs=(vmem, vmem),
        scratch_shapes=scratch,
        compiler_params=pltpu.CompilerParams(
            collective_id=0, has_side_effects=True, vmem_limit_bytes=58 * 2**20
        ),
        name="impute_and_sketch",
    )(ratings, observed, pool, neighbours.T, test_matrix)


def solution(mesh):
    in_specs = (
        P("users", "items"),
        P("users", "items"),
        P("users", "items"),
        P("users", None),
        P("users", None),
    )
    out_specs = (P("users", "items"), P("users", "items"))
    return jax.shard_map(body, mesh=mesh, in_specs=in_specs, out_specs=out_specs, check_vma=False)
```
